32 devices in a mesh: wave: 16 (over z, y, x), lev: 2 (over core).
Axes of the slice: x: 2, y: 2, z: 4, core: 2. Of those that a mesh axis runs over, the one named last changes fastest.
Arguments:
- fourier_in: bfloat16 [3, 28, 1280, 64], P(None, 'lev', 'wave'), may hold values from -6 to 6
- spectral_old: bfloat16 [3, 28, 16, 2816], P(None, 'lev', 'wave'), may hold values from -6 to 6
- legendre: bfloat16 [16, 1408, 1280], P('wave'), may hold values from -0.15625 to 0.15625
- g_matrix: float32 [28, 28], replicated, may hold values from -1 to 1
- modes_in: float32 [28, 28], replicated, may hold values from -1 to 1
- modes_out: float32 [28, 28], replicated, may hold values from -1 to 1
- mode_heating: float32 [28, 28], replicated, may hold values from -1 to 1
- mode_rates: float32 [28], replicated, may hold values from 0.1 to 10
- pair_ids: int32 [16], replicated, may hold values from 0 to 639, as said below
- lat_ids: int32 [1280], replicated, may hold values from 0 to 1279, each once
- limits: int32 [1280], replicated, may hold values from 10 to 1280
Outputs:
- spectral_new: bfloat16 [3, 28, 16, 2816], P(None, 'lev', 'wave')
- fourier_out: bfloat16 [3, 28, 1280, 64], P(None, 'lev', 'wave')
The draws below stay inside these ranges and needn't reach their ends.
Inputs may be any that keep to these rules, and one draw needn't show every extreme that they name: `pair_ids`: distinct pair numbers. `lat_ids`: each latitude once.
All inputs are finite; a program needn't handle non-finite values.
Results may differ from the reference program's by a relative error of at most 0.018.
Values may be sent and summed in bfloat16 or wider, within the bound.
A program may use at most 64 MiB of HBM per device.

```python
import math
import jax
import jax.numpy as jnp
from jax import lax

MMAX = 1280
NLAT = 1280
BLOCK = 64
LEV_DEV = 14
NR = 1408
NPW = 16
LEV = 28
N_LEV = 2


def draw_pair_ids(key, part):
    middle_ids = jax.random.permutation(key, MMAX // 2 - 2)[:NPW - 2].astype(jnp.int32) + 1
    end_ids = jnp.array([0, MMAX // 2 - 1], dtype=jnp.int32)
    chosen = jnp.concatenate([end_ids, middle_ids])
    shuffle = jax.random.permutation(jax.random.fold_in(key, 7), NPW)
    return chosen[shuffle]


def draw_limits(key, part):
    row_index = jnp.arange(NLAT, dtype=jnp.int32)
    from_pole = jnp.minimum(row_index, NLAT - 1 - row_index)
    jitter = jax.random.randint(key, (NLAT,), 0, 8, dtype=jnp.int32) * (from_pole > 0).astype(jnp.int32)
    return jnp.minimum(MMAX, 10 + 2 * from_pole + jitter).astype(jnp.int32)


def level_of(rng, extent, split, smallest, top_value):
    def one(axis_at, parts):
        draws = jax.random.uniform(jax.random.fold_in(jax.random.fold_in(rng, 6), axis_at), (parts,), jnp.float32, smallest / len(split), top_value / len(split))
        return jnp.repeat(jnp.exp(draws), extent[axis_at] // parts).reshape((-1,) + (1,) * (len(extent) - axis_at - 1))

    level = one(*split[0])
    for cut in split[1:]:
        level = level * one(*cut)
    return level


def centred(rng, extent, width, bound, shards=(), held_as=jnp.bfloat16):
    result = width * jax.random.normal(rng, extent, jnp.float32)
    if shards:
        result = result * level_of(rng, extent, shards, -0.22, 0.18)
    return jnp.clip(result, -bound, bound).astype(held_as)


def setup_inputs(seed: int = 0) -> dict:
    key_list = jax.random.split(jax.random.key(seed), 12)
    fourier_in = centred(key_list[0], (3, LEV, NLAT, 4 * NPW), 1.0, 6.0, ((1, 2), (2, 16)))
    spectral_old = centred(key_list[1], (3, LEV, NPW, 2 * NR), 1.0, 6.0, ((1, 2), (2, 16)))
    legendre = centred(key_list[2], (NPW, NR, NLAT), NLAT ** -0.5, 0.15625, ((0, 16),))
    g_matrix = centred(key_list[3], (LEV, LEV), LEV ** -0.5, 1.0, (), jnp.float32)
    modes_in = centred(key_list[4], (LEV, LEV), LEV ** -0.5, 1.0, (), jnp.float32)
    modes_out = centred(key_list[5], (LEV, LEV), LEV ** -0.5, 1.0, (), jnp.float32)
    mode_heating = centred(key_list[6], (LEV, LEV), LEV ** -0.5, 1.0, (), jnp.float32)
    mode_rates = jnp.clip(jnp.exp(jax.random.uniform(key_list[7], (LEV,), jnp.float32, math.log(0.1), math.log(10.0))), 0.1, 10.0)
    pair_ids = draw_pair_ids(jax.random.fold_in(key_list[11], 71), 0)
    lat_ids = jax.random.permutation(key_list[9], NLAT).astype(jnp.int32)
    limits = draw_limits(jax.random.fold_in(key_list[11], 71), 0)
    return dict(fourier_in=fourier_in, spectral_old=spectral_old, legendre=legendre, g_matrix=g_matrix, modes_in=modes_in, modes_out=modes_out, mode_heating=mode_heating, mode_rates=mode_rates, pair_ids=pair_ids, lat_ids=lat_ids, limits=limits)


coupling = 2.0
highest = lax.Precision.HIGHEST


def pair_layout(pair_number, row_count):
    row_index = jnp.arange(row_count, dtype=jnp.int32)
    first_length = MMAX - pair_number
    first_pad = ((first_length + BLOCK - 1) // BLOCK) * BLOCK
    in_first = row_index < first_pad
    row_valid = jnp.where(in_first, row_index < first_length, row_index - first_pad < pair_number + 1)
    degree = jnp.where(in_first, pair_number + row_index, MMAX - 1 - pair_number + row_index - first_pad).astype(jnp.float32)
    lfactor = degree * (degree + 1.0) / float(MMAX * (MMAX - 1))
    return row_valid, lfactor, first_pad


def grouped_levels(matrix, vector, group_count, lev_count):
    matrix_groups = matrix.reshape(matrix.shape[0], group_count, lev_count)
    vector_groups = vector.reshape(group_count, lev_count, vector.shape[1])
    partials = jnp.einsum("ogl,glx->gox", matrix_groups, vector_groups, precision=highest, preferred_element_type=jnp.float32)
    partials = lax.optimization_barrier(partials.astype(jnp.bfloat16))
    return jnp.sum(partials.astype(jnp.float32), axis=0)


def reference(fourier_in, spectral_old, legendre, g_matrix, modes_in, modes_out, mode_heating, mode_rates, pair_ids, lat_ids, limits):
    row_count = MMAX + 2 * BLOCK
    row_valid, lfactor, first_pad = jax.vmap(lambda pair_number: pair_layout(pair_number, row_count))(pair_ids)
    in_first = jnp.arange(row_count, dtype=jnp.int32)[None, :] < first_pad[:, None]
    row_limit = limits[lat_ids]
    both_waves = jnp.stack([pair_ids, MMAX - 1 - pair_ids], axis=1)
    column_wave = jnp.repeat(both_waves, 2, axis=1).reshape(-1)
    keep_mask = column_wave[None, :] < row_limit[:, None]
    masked = jnp.where(keep_mask[None, None], fourier_in, jnp.zeros((), fourier_in.dtype))
    slot_major = jnp.moveaxis(masked.reshape(3, LEV, NLAT, NPW, 2, 2), 3, 0)

    def forward_slot(operands):
        slot_data, pair_table, slot_first, slot_valid = operands
        table_wide = pair_table.astype(jnp.float32)
        data_wide = slot_data.astype(jnp.float32)
        first_wave = jnp.einsum("fljc,rj->flcr", data_wide[:, :, :, 0], table_wide, precision=highest)
        second_wave = jnp.einsum("fljc,rj->flcr", data_wide[:, :, :, 1], table_wide, precision=highest)
        chosen = jnp.where(slot_first[None, None, None, :], first_wave, second_wave)
        return jnp.where(slot_valid[None, None, None, :], chosen, 0.0)

    tendency = lax.map(forward_slot, (slot_major, legendre, in_first, row_valid))
    tendency = jnp.moveaxis(tendency, 0, 2)
    flat_size = NPW * 2 * row_count
    old_fields = spectral_old.reshape(3, LEV, NPW, 2, row_count).astype(jnp.float32)
    vorticity = (old_fields[0] + tendency[0]).reshape(LEV, flat_size)
    divergence = (old_fields[1] + tendency[1]).reshape(LEV, flat_size)
    heat_star = (old_fields[2] + tendency[2]).reshape(LEV, flat_size)
    wave_factor = jnp.broadcast_to(lfactor[:, None, :], (NPW, 2, row_count)).reshape(1, flat_size)
    keep_rows = jnp.broadcast_to(row_valid[:, None, :], (NPW, 2, row_count)).reshape(1, flat_size)
    hydrostatic = grouped_levels(g_matrix, heat_star, N_LEV, LEV_DEV)
    right_side = divergence + coupling * wave_factor * hydrostatic
    projected = grouped_levels(modes_in, right_side, N_LEV, LEV_DEV)
    modal_part = projected / (1.0 + coupling * coupling * wave_factor * mode_rates[:, None])
    divergence_new = grouped_levels(modes_out, modal_part, N_LEV, LEV_DEV)
    heat_change = grouped_levels(mode_heating, modal_part, N_LEV, LEV_DEV)
    vorticity_out = jnp.where(keep_rows, vorticity, 0.0).astype(jnp.bfloat16)
    divergence_out = jnp.where(keep_rows, divergence_new, 0.0).astype(jnp.bfloat16)
    heat_out = jnp.where(keep_rows, heat_star - coupling * heat_change, 0.0).astype(jnp.bfloat16)
    spectral_new = jnp.stack([vorticity_out, divergence_out, heat_out]).reshape(3, LEV, NPW, 2 * row_count)
    new_slots = jnp.moveaxis(spectral_new.reshape(3, LEV, NPW, 2, row_count), 2, 0)

    def inverse_slot(operands):
        slot_spectra, pair_table, slot_first = operands
        spectra_wide = slot_spectra.astype(jnp.float32)
        table_wide = pair_table.astype(jnp.float32)
        first_rows = jnp.where(slot_first[None, None, None, :], spectra_wide, 0.0)
        second_rows = jnp.where(jnp.logical_not(slot_first)[None, None, None, :], spectra_wide, 0.0)
        first_wave = jnp.einsum("flcr,rj->fljc", first_rows, table_wide, precision=highest)
        second_wave = jnp.einsum("flcr,rj->fljc", second_rows, table_wide, precision=highest)
        return jnp.stack([first_wave, second_wave], axis=3).reshape(3, LEV, NLAT, 4)

    gridded = lax.map(inverse_slot, (new_slots, legendre, in_first))
    gridded = jnp.moveaxis(gridded, 0, 3).reshape(3, LEV, NLAT, 4 * NPW)
    fourier_out = jnp.where(keep_mask[None, None], gridded, 0.0).astype(jnp.bfloat16)
    return (spectral_new, fourier_out)
```

```python
import functools

import jax
import jax.numpy as jnp
from jax import lax
from jax.experimental import pallas as pl
from jax.experimental.pallas import tpu as pltpu
from jax.sharding import PartitionSpec as P

MMAX = 1280
BLOCK = 64
K = 4
F32, BF16 = jnp.float32, jnp.bfloat16
MESH = pl.DeviceIdType.MESH
HI = lax.Precision.HIGHEST
NT = (((1,), (1,)), ((), ()))


def iota(shape, dim):
    return lax.broadcasted_iota(jnp.int32, shape, dim)


def dot(a, b):
    return jnp.dot(a, b, preferred_element_type=F32)


def fdot(a, b):
    return jnp.dot(a, b, precision=HI, preferred_element_type=F32)


def onehot(mask, dtype=BF16):
    return jnp.where(mask, 1.0, 0.0).astype(dtype)


def split3(left, right):
    lh = left.astype(BF16)
    ll = (left - lh.astype(F32)).astype(BF16)
    rh = right.astype(BF16)
    rl = (right - rh.astype(F32)).astype(BF16)
    return jnp.concatenate([lh, lh, ll], axis=1), jnp.concatenate([rh, rl, rh], axis=0)


def kernel(
    n, nlev, x_ref, old_ref, leg_hbm, g_ref, mi_ref, mo_ref, mh_ref, rates_ref, pid_ref, lat_ref, lim_ref,
    spec_ref, out_ref,
    leg, send1, recv1, send2, recv2, es1, er1, es2, er2,
    leg_sem, s1, r1, s2, r2, es, er,
):
    lev_n = x_ref.shape[1]
    fl_n = x_ref.shape[0] * lev_n
    q_n, jl = x_ref.shape[2], x_ref.shape[3]
    groups = (fl_n + K - 1) // K
    rows = groups * 16
    trows = groups * 8
    lanes = send1.shape[2]
    nr = leg_hbm.shape[1]
    nlat = leg_hbm.shape[2]
    first_mid = lev_n // K * 8
    mid = trows - first_mid
    half = er1.shape[0]
    me, lev = lax.axis_index("wave"), lax.axis_index("lev")
    other = lax.rem(lev + 1, nlev)

    leg_copy = pltpu.make_async_copy(leg_hbm.at[0], leg, leg_sem)
    leg_copy.start()

    barrier = pltpu.get_barrier_semaphore()

    def greet(i, carry):
        pl.semaphore_signal(barrier, inc=1, device_id=(lax.rem(me + i, n), lev), device_id_type=MESH)
        return carry

    lax.fori_loop(1, n, greet, 0)
    pl.semaphore_signal(barrier, inc=1, device_id=(me, other), device_id_type=MESH)

    col = iota((jl, nlat), 1)
    own = jnp.sum(jnp.where(col == me * jl + iota((jl, nlat), 0), lat_ref[...], 0.0), axis=1, keepdims=True)
    lim = jnp.sum(jnp.where(col.astype(F32) == own, lim_ref[...], 0.0), axis=1, keepdims=True)
    lim = jnp.sum(jnp.where(iota((jl, jl), 0) == iota((jl, jl), 1), lim, 0.0), axis=0, keepdims=True)
    q = iota((q_n, jl), 0)
    slot = q // 4
    pair = jnp.zeros((q_n, jl), jnp.int32)
    for s in range(n):
        pair = jnp.where(slot == s, pid_ref[s], pair)
    wave = jnp.where(q // 2 % 2 == 0, pair, MMAX - 1 - pair)
    keep = onehot(wave.astype(F32) < lim, F32)

    pr, pc = iota((K * q_n, K * q_n), 0), iota((K * q_n, K * q_n), 1)
    perm = onehot(pc == pr % K * q_n + pr // K)
    keep_b = keep.astype(BF16)
    pieces = []
    for k in range(K):
        parts = []
        for g in range(groups):
            fl = g * K + k
            if fl < fl_n:
                parts.append(x_ref[fl // lev_n, fl % lev_n] * keep_b)
            else:
                parts.append(jnp.zeros((q_n, jl), BF16))
        if lanes > groups * jl:
            parts.append(jnp.zeros((q_n, lanes - groups * jl), BF16))
        pieces.append(jnp.concatenate(parts, axis=1))
    send1[...] = dot(perm, jnp.concatenate(pieces, axis=0)).astype(BF16).reshape(n, 16, lanes)

    pl.semaphore_wait(barrier, n)

    def copy1(i):
        to = lax.rem(me + i, n)
        return pltpu.make_async_remote_copy(
            src_ref=send1.at[to], dst_ref=recv1.at[me], send_sem=s1.at[to], recv_sem=r1.at[me],
            device_id=(to, lev), device_id_type=MESH,
        )

    def start1(i, carry):
        copy1(i).start()
        return carry

    lax.fori_loop(1, n, start1, 0)
    recv1[me] = send1[me]

    a = pid_ref[me]
    r = iota((1, nr), 1)
    first_pad = (MMAX - a + BLOCK - 1) // BLOCK * BLOCK
    first = r < first_pad
    used = (first & (r < MMAX - a)) | ((r >= first_pad) & (r - first_pad <= a))
    degree = jnp.where(first, a + r, MMAX - 1 - a + r - first_pad).astype(F32)
    lam = degree * (degree + 1.0) / float(MMAX * (MMAX - 1))

    tr, tc = iota((trows, fl_n), 0), iota((trows, fl_n), 1)
    tfl = tr // 8 * K + tr % K
    old = jnp.concatenate([old_ref[f, 0] for f in range(3)], axis=0)
    old_rows = sum(
        dot(onehot((tfl == tc) & (tr // 4 % 2 == c)), old[:, c * nr : (c + 1) * nr]) for c in range(2)
    )

    def mid_row(i):
        i = i + first_mid
        fl = i // 8 * K + i % K
        return fl // lev_n, fl % lev_n, i // 4 % 2

    levels = nlev * lev_n

    def mode_of(i, h):
        return lev_n * ((lev + h) % nlev) + i // 2

    i1, o1 = iota((2 * half, levels), 0), iota((2 * half, levels), 1)
    pick_out = onehot((o1 == mode_of(i1 % half, i1 // half)) & (i1 % half < 2 * lev_n), F32)
    field, level, cc = mid_row(iota((levels, mid), 1))
    pick_in = onehot(iota((levels, mid), 0) == lev_n * lev + level, F32)
    field, level, cc = mid_row(iota((2 * half, mid), 1))
    same_c = iota((2 * half, mid), 0) % 2 == cc
    m_in = mi_ref[...]
    w_div = jnp.where(same_c & (field == 1), fdot(fdot(pick_out, m_in), pick_in), 0.0)
    w_heat = jnp.where(same_c & (field == 2), fdot(fdot(pick_out, fdot(m_in, g_ref[...])), pick_in), 0.0)
    w1 = jnp.concatenate([w_div, w_heat], axis=0)
    im, om = iota((half, levels), 0), iota((half, levels), 1)
    own_mode = (om == lev_n * lev + im // 2) & (im < 2 * lev_n)
    rates = jnp.sum(jnp.where(own_mode, rates_ref[...], 0.0), axis=1, keepdims=True)
    i2, l2 = iota((2 * mid, levels), 0), iota((2 * mid, levels), 1)
    field, level, cc = mid_row(i2 % mid)
    pick_lev = onehot(l2 == lev_n * ((lev + i2 // mid) % nlev) + level, F32)
    im, om = iota((levels, half), 1), iota((levels, half), 0)
    pick_mode = onehot((om == lev_n * lev + im // 2) & (im < 2 * lev_n), F32)
    field, level, cc = mid_row(iota((2 * mid, half), 0) % mid)
    same_c = iota((2 * mid, half), 1) % 2 == cc
    w2 = jnp.where(same_c & (field == 1), fdot(fdot(pick_lev, mo_ref[...]), pick_mode), 0.0)
    w2 = w2 + jnp.where(same_c & (field == 2), -2.0 * fdot(fdot(pick_lev, mh_ref[...]), pick_mode), 0.0)
    field, level, cc = mid_row(iota((mid, 1), 0))
    stays = onehot(field != 1, F32)

    leg_copy.wait()

    def wait1(i, carry):
        copy1(i).wait_send()
        frm = lax.rem(me + n - i, n)
        pltpu.make_async_remote_copy(
            src_ref=send1.at[frm], dst_ref=recv1.at[frm], send_sem=s1.at[frm], recv_sem=r1.at[frm],
            device_id=(frm, lev), device_id_type=MESH,
        ).wait_recv()
        return carry

    lax.fori_loop(1, n, wait1, 0)

    cols = jnp.concatenate(
        [
            jnp.concatenate([recv1[d, :, g * jl : (g + 1) * jl] for d in range(n)], axis=1)
            for g in range(groups)
        ],
        axis=0,
    )
    both = lax.dot_general(cols, leg[...], NT, preferred_element_type=F32).reshape(groups, 2, 8, nr)
    total = jnp.where(iota((groups, 8, nr), 2) < first_pad, both[:, 0], both[:, 1])
    total = old_rows + jnp.where(used, total.reshape(trows, nr), 0.0)

    def exchange(src, dst, k):
        return pltpu.make_async_remote_copy(
            src_ref=src, dst_ref=dst, send_sem=es.at[k], recv_sem=er.at[k],
            device_id=(me, other), device_id_type=MESH,
        )

    tmid = total[first_mid:]
    w1s, t1s = split3(w1, tmid)
    res = dot(w1s, t1s)
    proj = res[: 2 * half] + 2.0 * lam * res[2 * half :]
    es1[...] = proj[half:].astype(BF16)
    exchange(es1, er1, 0).start()
    exchange(es1, er1, 0).wait()
    modal = (proj[:half] + er1[...].astype(F32)) / (1.0 + 4.0 * lam * rates)
    w2s, m2s = split3(w2, modal)
    res = dot(w2s, m2s)
    es2[...] = res[mid:].astype(BF16)
    exchange(es2, er2, 1).start()
    exchange(es2, er2, 1).wait()
    new_mid = tmid * stays + res[:mid] + er2[...].astype(F32)
    new = jnp.concatenate([total[:first_mid], new_mid], axis=0) if first_mid else new_mid
    new = jnp.where(used, new, 0.0)
    sides = jnp.stack(
        [
            jnp.where(first, new, 0.0).reshape(groups, 8, nr),
            jnp.where(first, 0.0, new).reshape(groups, 8, nr),
        ],
        axis=1,
    ).reshape(rows, nr).astype(BF16)
    grid = dot(sides, leg[...]).astype(BF16)
    for d in range(n):
        parts = [grid[g * 16 : (g + 1) * 16, d * jl : (d + 1) * jl] for g in range(groups)]
        if lanes > groups * jl:
            parts.append(jnp.zeros((16, lanes - groups * jl), BF16))
        send2[d] = jnp.concatenate(parts, axis=1)

    def copy2(i):
        to = lax.rem(me + i, n)
        return pltpu.make_async_remote_copy(
            src_ref=send2.at[to], dst_ref=recv2.at[me], send_sem=s2.at[to], recv_sem=r2.at[me],
            device_id=(to, lev), device_id_type=MESH,
        )

    def start2(i, carry):
        copy2(i).start()
        return carry

    lax.fori_loop(1, n, start2, 0)
    recv2[me] = send2[me]

    new_b = new.astype(BF16)
    sr, sc = iota((fl_n, trows), 0), iota((fl_n, trows), 1)
    sfl = sc // 8 * K + sc % K
    for c in range(2):
        part = dot(onehot((sfl == sr) & (sc // 4 % 2 == c)), new_b).astype(BF16)
        for f in range(3):
            spec_ref[f, 0, :, c * nr : (c + 1) * nr] = part[f * lev_n : (f + 1) * lev_n]

    def wait2(i, carry):
        copy2(i).wait_send()
        frm = lax.rem(me + n - i, n)
        pltpu.make_async_remote_copy(
            src_ref=send2.at[frm], dst_ref=recv2.at[frm], send_sem=s2.at[frm], recv_sem=r2.at[frm],
            device_id=(frm, lev), device_id_type=MESH,
        ).wait_recv()
        return carry

    lax.fori_loop(1, n, wait2, 0)
    perm_back = onehot(pr == pc % K * q_n + pc // K)
    back = dot(perm_back, recv2[...].reshape(K * q_n, lanes))
    for g in range(groups):
        for k in range(K):
            fl = g * K + k
            if fl < fl_n:
                piece = back[k * q_n : (k + 1) * q_n, g * jl : (g + 1) * jl] * keep
                out_ref[fl // lev_n, fl % lev_n] = piece.astype(BF16)


def body(
    fourier_in, spectral_old, legendre, g_matrix, modes_in, modes_out, mode_heating, mode_rates, pair_ids, lat_ids,
    limits,
):
    n, nlev = lax.axis_size("wave"), lax.axis_size("lev")
    fields, lev_n, jl, q_n = fourier_in.shape
    groups = (fields * lev_n + K - 1) // K
    lanes = (groups * jl + 127) // 128 * 128
    nr, nlat = legendre.shape[1:]
    half = (2 * lev_n + 15) // 16 * 16
    mid = groups * 8 - lev_n // K * 8
    vmem = pl.BlockSpec(memory_space=pltpu.VMEM)
    spec, out = pl.pallas_call(
        functools.partial(kernel, n, nlev),
        out_shape=(
            jax.ShapeDtypeStruct((fields, 1, lev_n, 2 * nr), BF16),
            jax.ShapeDtypeStruct((fields, lev_n, q_n, jl), BF16),
        ),
        in_specs=[vmem, vmem, pl.BlockSpec(memory_space=pl.ANY)] + [vmem] * 5
        + [pl.BlockSpec(memory_space=pltpu.SMEM)] + [vmem] * 2,
        out_specs=(vmem, vmem),
        scratch_shapes=[
            pltpu.VMEM((nr, nlat), BF16),
            pltpu.VMEM((n, 16, lanes), BF16),
            pltpu.VMEM((n, 16, lanes), BF16),
            pltpu.VMEM((n, 16, lanes), BF16),
            pltpu.VMEM((n, 16, lanes), BF16),
            pltpu.VMEM((half, nr), BF16),
            pltpu.VMEM((half, nr), BF16),
            pltpu.VMEM((mid, nr), BF16),
            pltpu.VMEM((mid, nr), BF16),
            pltpu.SemaphoreType.DMA,
            pltpu.SemaphoreType.DMA((n,)),
            pltpu.SemaphoreType.DMA((n,)),
            pltpu.SemaphoreType.DMA((n,)),
            pltpu.SemaphoreType.DMA((n,)),
            pltpu.SemaphoreType.DMA((2,)),
            pltpu.SemaphoreType.DMA((2,)),
        ],
        compiler_params=pltpu.CompilerParams(
            collective_id=0, has_side_effects=True, vmem_limit_bytes=48 * 1024 * 1024
        ),
        cost_estimate=pl.CostEstimate(flops=10**9, bytes_accessed=8 * 10**6, transcendentals=0),
    )(
        jnp.transpose(fourier_in, (0, 1, 3, 2)),
        jnp.transpose(spectral_old, (0, 2, 1, 3)),
        legendre,
        g_matrix,
        modes_in,
        modes_out,
        mode_heating,
        mode_rates[None, :],
        pair_ids,
        lat_ids.astype(F32)[None, :],
        limits.astype(F32)[None, :],
    )
    return jnp.transpose(spec, (0, 2, 1, 3)), jnp.transpose(out, (0, 1, 3, 2))


def solution(mesh):
    wave = P(None, "lev", "wave", None)
    return jax.shard_map(
        body,
        mesh=mesh,
        in_specs=(wave, wave, P("wave", None, None)) + (P(),) * 8,
        out_specs=(wave, wave),
        check_vma=False,
    )
```

```python
import functools

import jax
import jax.numpy as jnp
from jax import lax
from jax.experimental import pallas as pl
from jax.experimental.pallas import tpu as pltpu
from jax.sharding import PartitionSpec as P

MMAX = 1280
BLOCK = 64
K = 4
F32, BF16 = jnp.float32, jnp.bfloat16
MESH = pl.DeviceIdType.MESH
HI = lax.Precision.HIGHEST
NT = (((1,), (1,)), ((), ()))


def iota(shape, dim):
    return lax.broadcasted_iota(jnp.int32, shape, dim)


def dot(a, b):
    return jnp.dot(a, b, preferred_element_type=F32)


def fdot(a, b):
    return jnp.dot(a, b, precision=HI, preferred_element_type=F32)


def onehot(mask, dtype=BF16):
    return jnp.where(mask, 1.0, 0.0).astype(dtype)


def split3(left, right):
    lh = left.astype(BF16)
    ll = (left - lh.astype(F32)).astype(BF16)
    rh = right.astype(BF16)
    rl = (right - rh.astype(F32)).astype(BF16)
    return jnp.concatenate([lh, lh, ll], axis=1), jnp.concatenate([rh, rl, rh], axis=0)


def kernel(
    n, nlev, x_hbm, old_hbm, leg_hbm, g_hbm, mi_hbm, mo_hbm, mh_hbm, rates_hbm, pid_hbm, lat_hbm, lim_hbm,
    spec_ref, out_ref,
    x_ref, old_ref, leg, g_ref, mi_ref, mo_ref, mh_ref, rates_ref, pid_ref, lat_ref, lim_ref,
    send1, recv1, send2, recv2, es1, er1, es2, er2,
    in_sem, s1, r1, s2, r2, es, er,
):
    lev_n = x_ref.shape[1]
    fl_n = x_ref.shape[0] * lev_n
    q_n, jl = x_ref.shape[2], x_ref.shape[3]
    groups = (fl_n + K - 1) // K
    rows = groups * 16
    trows = groups * 8
    lanes = send1.shape[2]
    nr = leg_hbm.shape[1]
    nlat = leg_hbm.shape[2]
    first_mid = lev_n // K * 8
    mid = trows - first_mid
    half = er1.shape[0]
    me, lev = lax.axis_index("wave"), lax.axis_index("lev")
    other = lax.rem(lev + 1, nlev)

    pairs = [
        (pid_hbm, pid_ref), (lat_hbm, lat_ref), (lim_hbm, lim_ref), (x_hbm, x_ref), (g_hbm, g_ref), (mi_hbm, mi_ref),
        (mo_hbm, mo_ref), (mh_hbm, mh_ref), (rates_hbm, rates_ref), (old_hbm, old_ref), (leg_hbm.at[0], leg),
    ]
    loads = [pltpu.make_async_copy(src, dst, in_sem.at[i]) for i, (src, dst) in enumerate(pairs)]
    for load in loads:
        load.start()

    barrier = pltpu.get_barrier_semaphore()

    def greet(i, carry):
        pl.semaphore_signal(barrier, inc=1, device_id=(lax.rem(me + i, n), lev), device_id_type=MESH)
        return carry

    lax.fori_loop(1, n, greet, 0)
    pl.semaphore_signal(barrier, inc=1, device_id=(me, other), device_id_type=MESH)

    for load in loads[:4]:
        load.wait()

    col = iota((jl, nlat), 1)
    own = jnp.sum(jnp.where(col == me * jl + iota((jl, nlat), 0), lat_ref[...].astype(F32)[None, :], 0.0), axis=1, keepdims=True)
    lim = jnp.sum(jnp.where(col.astype(F32) == own, lim_ref[...].astype(F32)[None, :], 0.0), axis=1, keepdims=True)
    lim = jnp.sum(jnp.where(iota((jl, jl), 0) == iota((jl, jl), 1), lim, 0.0), axis=0, keepdims=True)
    q = iota((q_n, jl), 0)
    slot = q // 4
    pair = jnp.zeros((q_n, jl), jnp.int32)
    for s in range(n):
        pair = jnp.where(slot == s, pid_ref[s], pair)
    wave = jnp.where(q // 2 % 2 == 0, pair, MMAX - 1 - pair)
    keep = onehot(wave.astype(F32) < lim, F32)

    pr, pc = iota((K * q_n, K * q_n), 0), iota((K * q_n, K * q_n), 1)
    perm = onehot(pc == pr % K * q_n + pr // K)
    keep_b = keep.astype(BF16)
    pieces = []
    for k in range(K):
        parts = []
        for g in range(groups):
            fl = g * K + k
            if fl < fl_n:
                parts.append(x_ref[fl // lev_n, fl % lev_n] * keep_b)
            else:
                parts.append(jnp.zeros((q_n, jl), BF16))
        if lanes > groups * jl:
            parts.append(jnp.zeros((q_n, lanes - groups * jl), BF16))
        pieces.append(jnp.concatenate(parts, axis=1))
    send1[...] = dot(perm, jnp.concatenate(pieces, axis=0)).astype(BF16).reshape(n, 16, lanes)

    pl.semaphore_wait(barrier, n)

    def copy1(i):
        to = lax.rem(me + i, n)
        return pltpu.make_async_remote_copy(
            src_ref=send1.at[to], dst_ref=recv1.at[me], send_sem=s1.at[to], recv_sem=r1.at[me],
            device_id=(to, lev), device_id_type=MESH,
        )

    def start1(i, carry):
        copy1(i).start()
        return carry

    lax.fori_loop(1, n, start1, 0)
    recv1[me] = send1[me]

    for load in loads[4:10]:
        load.wait()
    a = pid_ref[me]
    r = iota((1, nr), 1)
    first_pad = (MMAX - a + BLOCK - 1) // BLOCK * BLOCK
    first = r < first_pad
    used = (first & (r < MMAX - a)) | ((r >= first_pad) & (r - first_pad <= a))
    degree = jnp.where(first, a + r, MMAX - 1 - a + r - first_pad).astype(F32)
    lam = degree * (degree + 1.0) / float(MMAX * (MMAX - 1))

    tr, tc = iota((trows, fl_n), 0), iota((trows, fl_n), 1)
    tfl = tr // 8 * K + tr % K
    old = jnp.concatenate([old_ref[f, 0] for f in range(3)], axis=0)
    old_rows = sum(
        dot(onehot((tfl == tc) & (tr // 4 % 2 == c)), old[:, c * nr : (c + 1) * nr]) for c in range(2)
    )

    def mid_row(i):
        i = i + first_mid
        fl = i // 8 * K + i % K
        return fl // lev_n, fl % lev_n, i // 4 % 2

    levels = nlev * lev_n

    def mode_of(i, h):
        return lev_n * ((lev + h) % nlev) + i // 2

    i1, o1 = iota((2 * half, levels), 0), iota((2 * half, levels), 1)
    pick_out = onehot((o1 == mode_of(i1 % half, i1 // half)) & (i1 % half < 2 * lev_n), F32)
    field, level, cc = mid_row(iota((levels, mid), 1))
    pick_in = onehot(iota((levels, mid), 0) == lev_n * lev + level, F32)
    field, level, cc = mid_row(iota((2 * half, mid), 1))
    same_c = iota((2 * half, mid), 0) % 2 == cc
    m_in = mi_ref[...]
    w_div = jnp.where(same_c & (field == 1), fdot(fdot(pick_out, m_in), pick_in), 0.0)
    w_heat = jnp.where(same_c & (field == 2), fdot(fdot(pick_out, fdot(m_in, g_ref[...])), pick_in), 0.0)
    w1 = jnp.concatenate([w_div, w_heat], axis=0)
    im, om = iota((half, levels), 0), iota((half, levels), 1)
    own_mode = (om == lev_n * lev + im // 2) & (im < 2 * lev_n)
    rates = jnp.sum(jnp.where(own_mode, rates_ref[...][None, :], 0.0), axis=1, keepdims=True)
    i2, l2 = iota((2 * mid, levels), 0), iota((2 * mid, levels), 1)
    field, level, cc = mid_row(i2 % mid)
    pick_lev = onehot(l2 == lev_n * ((lev + i2 // mid) % nlev) + level, F32)
    im, om = iota((levels, half), 1), iota((levels, half), 0)
    pick_mode = onehot((om == lev_n * lev + im // 2) & (im < 2 * lev_n), F32)
    field, level, cc = mid_row(iota((2 * mid, half), 0) % mid)
    same_c = iota((2 * mid, half), 1) % 2 == cc
    w2 = jnp.where(same_c & (field == 1), fdot(fdot(pick_lev, mo_ref[...]), pick_mode), 0.0)
    w2 = w2 + jnp.where(same_c & (field == 2), -2.0 * fdot(fdot(pick_lev, mh_ref[...]), pick_mode), 0.0)
    field, level, cc = mid_row(iota((mid, 1), 0))
    stays = onehot(field != 1, F32)

    loads[10].wait()

    def wait1(i, carry):
        copy1(i).wait_send()
        frm = lax.rem(me + n - i, n)
        pltpu.make_async_remote_copy(
            src_ref=send1.at[frm], dst_ref=recv1.at[frm], send_sem=s1.at[frm], recv_sem=r1.at[frm],
            device_id=(frm, lev), device_id_type=MESH,
        ).wait_recv()
        return carry

    lax.fori_loop(1, n, wait1, 0)

    cols = jnp.concatenate(
        [
            jnp.concatenate([recv1[d, :, g * jl : (g + 1) * jl] for d in range(n)], axis=1)
            for g in range(groups)
        ],
        axis=0,
    )
    both = lax.dot_general(cols, leg[...], NT, preferred_element_type=F32).reshape(groups, 2, 8, nr)
    total = jnp.where(iota((groups, 8, nr), 2) < first_pad, both[:, 0], both[:, 1])
    total = old_rows + jnp.where(used, total.reshape(trows, nr), 0.0)

    def exchange(src, dst, k):
        return pltpu.make_async_remote_copy(
            src_ref=src, dst_ref=dst, send_sem=es.at[k], recv_sem=er.at[k],
            device_id=(me, other), device_id_type=MESH,
        )

    tmid = total[first_mid:]
    w1s, t1s = split3(w1, tmid)
    res = dot(w1s, t1s)
    proj = res[: 2 * half] + 2.0 * lam * res[2 * half :]
    es1[...] = proj[half:].astype(BF16)
    exchange(es1, er1, 0).start()
    exchange(es1, er1, 0).wait()
    modal = (proj[:half] + er1[...].astype(F32)) / (1.0 + 4.0 * lam * rates)
    w2s, m2s = split3(w2, modal)
    res = dot(w2s, m2s)
    es2[...] = res[mid:].astype(BF16)
    exchange(es2, er2, 1).start()
    exchange(es2, er2, 1).wait()
    new_mid = tmid * stays + res[:mid] + er2[...].astype(F32)
    new = jnp.concatenate([total[:first_mid], new_mid], axis=0) if first_mid else new_mid
    new = jnp.where(used, new, 0.0)
    sides = jnp.stack(
        [
            jnp.where(first, new, 0.0).reshape(groups, 8, nr),
            jnp.where(first, 0.0, new).reshape(groups, 8, nr),
        ],
        axis=1,
    ).reshape(rows, nr).astype(BF16)
    grid = dot(sides, leg[...]).astype(BF16)
    for d in range(n):
        parts = [grid[g * 16 : (g + 1) * 16, d * jl : (d + 1) * jl] for g in range(groups)]
        if lanes > groups * jl:
            parts.append(jnp.zeros((16, lanes - groups * jl), BF16))
        send2[d] = jnp.concatenate(parts, axis=1)

    def copy2(i):
        to = lax.rem(me + i, n)
        return pltpu.make_async_remote_copy(
            src_ref=send2.at[to], dst_ref=recv2.at[me], send_sem=s2.at[to], recv_sem=r2.at[me],
            device_id=(to, lev), device_id_type=MESH,
        )

    def start2(i, carry):
        copy2(i).start()
        return carry

    lax.fori_loop(1, n, start2, 0)
    recv2[me] = send2[me]

    new_b = new.astype(BF16)
    sr, sc = iota((fl_n, trows), 0), iota((fl_n, trows), 1)
    sfl = sc // 8 * K + sc % K
    for c in range(2):
        part = dot(onehot((sfl == sr) & (sc // 4 % 2 == c)), new_b).astype(BF16)
        for f in range(3):
            spec_ref[f, 0, :, c * nr : (c + 1) * nr] = part[f * lev_n : (f + 1) * lev_n]

    def wait2(i, carry):
        copy2(i).wait_send()
        frm = lax.rem(me + n - i, n)
        pltpu.make_async_remote_copy(
            src_ref=send2.at[frm], dst_ref=recv2.at[frm], send_sem=s2.at[frm], recv_sem=r2.at[frm],
            device_id=(frm, lev), device_id_type=MESH,
        ).wait_recv()
        return carry

    lax.fori_loop(1, n, wait2, 0)
    perm_back = onehot(pr == pc % K * q_n + pc // K)
    back = dot(perm_back, recv2[...].reshape(K * q_n, lanes))
    for g in range(groups):
        for k in range(K):
            fl = g * K + k
            if fl < fl_n:
                piece = back[k * q_n : (k + 1) * q_n, g * jl : (g + 1) * jl] * keep
                out_ref[fl // lev_n, fl % lev_n] = piece.astype(BF16)


def body(
    fourier_in, spectral_old, legendre, g_matrix, modes_in, modes_out, mode_heating, mode_rates, pair_ids, lat_ids,
    limits,
):
    n, nlev = lax.axis_size("wave"), lax.axis_size("lev")
    fields, lev_n, jl, q_n = fourier_in.shape
    groups = (fields * lev_n + K - 1) // K
    lanes = (groups * jl + 127) // 128 * 128
    nr, nlat = legendre.shape[1:]
    half = (2 * lev_n + 15) // 16 * 16
    mid = groups * 8 - lev_n // K * 8
    vmem = pl.BlockSpec(memory_space=pltpu.VMEM)
    spec, out = pl.pallas_call(
        functools.partial(kernel, n, nlev),
        out_shape=(
            jax.ShapeDtypeStruct((fields, 1, lev_n, 2 * nr), BF16),
            jax.ShapeDtypeStruct((fields, lev_n, q_n, jl), BF16),
        ),
        in_specs=[pl.BlockSpec(memory_space=pltpu.HBM)] * 11,
        out_specs=(vmem, vmem),
        scratch_shapes=[
            pltpu.VMEM((fields, lev_n, q_n, jl), BF16),
            pltpu.VMEM((fields, 1, lev_n, 2 * nr), BF16),
            pltpu.VMEM((nr, nlat), BF16),
            pltpu.VMEM(g_matrix.shape, F32),
            pltpu.VMEM(g_matrix.shape, F32),
            pltpu.VMEM(g_matrix.shape, F32),
            pltpu.VMEM(g_matrix.shape, F32),
            pltpu.VMEM(mode_rates.shape, F32),
            pltpu.SMEM(pair_ids.shape, jnp.int32),
            pltpu.VMEM(lat_ids.shape, jnp.int32),
            pltpu.VMEM(limits.shape, jnp.int32),
            pltpu.VMEM((n, 16, lanes), BF16),
            pltpu.VMEM((n, 16, lanes), BF16),
            pltpu.VMEM((n, 16, lanes), BF16),
            pltpu.VMEM((n, 16, lanes), BF16),
            pltpu.VMEM((half, nr), BF16),
            pltpu.VMEM((half, nr), BF16),
            pltpu.VMEM((mid, nr), BF16),
            pltpu.VMEM((mid, nr), BF16),
            pltpu.SemaphoreType.DMA((11,)),
            pltpu.SemaphoreType.DMA((n,)),
            pltpu.SemaphoreType.DMA((n,)),
            pltpu.SemaphoreType.DMA((n,)),
            pltpu.SemaphoreType.DMA((n,)),
            pltpu.SemaphoreType.DMA((2,)),
            pltpu.SemaphoreType.DMA((2,)),
        ],
        compiler_params=pltpu.CompilerParams(
            collective_id=0, has_side_effects=True, vmem_limit_bytes=63 * 1024 * 1024
        ),
        cost_estimate=pl.CostEstimate(flops=10**9, bytes_accessed=8 * 10**6, transcendentals=0),
    )(
        jnp.transpose(fourier_in, (0, 1, 3, 2)),
        jnp.transpose(spectral_old, (0, 2, 1, 3)),
        legendre,
        g_matrix,
        modes_in,
        modes_out,
        mode_heating,
        mode_rates,
        pair_ids,
        lat_ids,
        limits,
    )
    return jnp.transpose(spec, (0, 2, 1, 3)), jnp.transpose(out, (0, 1, 3, 2))


def solution(mesh):
    wave = P(None, "lev", "wave", None)
    return jax.shard_map(
        body,
        mesh=mesh,
        in_specs=(wave, wave, P("wave", None, None)) + (P(),) * 8,
        out_specs=(wave, wave),
        check_vma=False,
    )
```

```python
import functools

import jax
import jax.numpy as jnp
from jax import lax
from jax.experimental import pallas as pl
from jax.experimental.pallas import tpu as pltpu
from jax.sharding import PartitionSpec as P

MMAX = 1280
BLOCK = 64
K = 4
F32, BF16 = jnp.float32, jnp.bfloat16
MESH = pl.DeviceIdType.MESH
HI = lax.Precision.HIGHEST
NT = (((1,), (1,)), ((), ()))


def iota(shape, dim):
    return lax.broadcasted_iota(jnp.int32, shape, dim)


def dot(a, b):
    return jnp.dot(a, b, preferred_element_type=F32)


def fdot(a, b):
    return jnp.dot(a, b, precision=HI, preferred_element_type=F32)


def onehot(mask, dtype=BF16):
    return jnp.where(mask, 1.0, 0.0).astype(dtype)


def split3(left, right):
    lh = left.astype(BF16)
    ll = (left - lh.astype(F32)).astype(BF16)
    rh = right.astype(BF16)
    rl = (right - rh.astype(F32)).astype(BF16)
    return jnp.concatenate([lh, lh, ll], axis=1), jnp.concatenate([rh, rl, rh], axis=0)


def kernel(
    n, nlev, x_hbm, old_hbm, leg_hbm, g_hbm, mi_hbm, mo_hbm, mh_hbm, rates_hbm, pid_hbm, lat_hbm, lim_hbm,
    spec_hbm, out_hbm,
    spec_ref, out_ref, x_ref, old_ref, leg, g_ref, mi_ref, mo_ref, mh_ref, rates_ref, pid_ref, lat_ref, lim_ref,
    send1, recv1, send2, recv2, es1, er1, es2, er2,
    out_sem, in_sem, s1, r1, s2, r2, es, er,
):
    lev_n = x_ref.shape[1]
    fl_n = x_ref.shape[0] * lev_n
    q_n, jl = x_ref.shape[2], x_ref.shape[3]
    groups = (fl_n + K - 1) // K
    rows = groups * 16
    trows = groups * 8
    lanes = send1.shape[2]
    nr = leg_hbm.shape[1]
    nlat = leg_hbm.shape[2]
    first_mid = lev_n // K * 8
    mid = trows - first_mid
    half = er1.shape[0]
    me, lev = lax.axis_index("wave"), lax.axis_index("lev")
    other = lax.rem(lev + 1, nlev)

    pairs = [
        (pid_hbm, pid_ref), (lat_hbm, lat_ref), (lim_hbm, lim_ref), (x_hbm, x_ref), (g_hbm, g_ref), (mi_hbm, mi_ref),
        (mo_hbm, mo_ref), (mh_hbm, mh_ref), (rates_hbm, rates_ref), (old_hbm, old_ref), (leg_hbm.at[0], leg),
    ]
    loads = [pltpu.make_async_copy(src, dst, in_sem.at[i]) for i, (src, dst) in enumerate(pairs)]
    for load in loads:
        load.start()

    barrier = pltpu.get_barrier_semaphore()

    def greet(i, carry):
        pl.semaphore_signal(barrier, inc=1, device_id=(lax.rem(me + i, n), lev), device_id_type=MESH)
        return carry

    lax.fori_loop(1, n, greet, 0)
    pl.semaphore_signal(barrier, inc=1, device_id=(me, other), device_id_type=MESH)

    for load in loads[:4]:
        load.wait()

    col = iota((jl, nlat), 1)
    own = jnp.sum(jnp.where(col == me * jl + iota((jl, nlat), 0), lat_ref[...].astype(F32)[None, :], 0.0), axis=1, keepdims=True)
    lim = jnp.sum(jnp.where(col.astype(F32) == own, lim_ref[...].astype(F32)[None, :], 0.0), axis=1, keepdims=True)
    lim = jnp.sum(jnp.where(iota((jl, jl), 0) == iota((jl, jl), 1), lim, 0.0), axis=0, keepdims=True)
    q = iota((q_n, jl), 0)
    slot = q // 4
    pair = jnp.zeros((q_n, jl), jnp.int32)
    for s in range(n):
        pair = jnp.where(slot == s, pid_ref[s], pair)
    wave = jnp.where(q // 2 % 2 == 0, pair, MMAX - 1 - pair)
    keep = onehot(wave.astype(F32) < lim, F32)

    pr, pc = iota((K * q_n, K * q_n), 0), iota((K * q_n, K * q_n), 1)
    perm = onehot(pc == pr % K * q_n + pr // K)
    keep_b = keep.astype(BF16)
    pieces = []
    for k in range(K):
        parts = []
        for g in range(groups):
            fl = g * K + k
            if fl < fl_n:
                parts.append(x_ref[fl // lev_n, fl % lev_n] * keep_b)
            else:
                parts.append(jnp.zeros((q_n, jl), BF16))
        if lanes > groups * jl:
            parts.append(jnp.zeros((q_n, lanes - groups * jl), BF16))
        pieces.append(jnp.concatenate(parts, axis=1))
    send1[...] = dot(perm, jnp.concatenate(pieces, axis=0)).astype(BF16).reshape(n, 16, lanes)

    pl.semaphore_wait(barrier, n)

    hn = n // 2
    near, far = me // hn, 1 - me // hn

    def peer(side, i):
        return side * hn + lax.rem(me + i, hn)

    def copy1(to):
        return pltpu.make_async_remote_copy(
            src_ref=send1.at[to], dst_ref=recv1.at[me], send_sem=s1.at[to], recv_sem=r1.at[me],
            device_id=(to, lev), device_id_type=MESH,
        )

    def start1(side):
        def step(i, carry):
            copy1(peer(side, i)).start()
            return carry

        return step

    lax.fori_loop(0, hn, start1(far), 0)
    lax.fori_loop(1, hn, start1(near), 0)
    recv1[me] = send1[me]

    for load in loads[4:10]:
        load.wait()
    a = pid_ref[me]
    r = iota((1, nr), 1)
    first_pad = (MMAX - a + BLOCK - 1) // BLOCK * BLOCK
    first = r < first_pad
    used = (first & (r < MMAX - a)) | ((r >= first_pad) & (r - first_pad <= a))
    degree = jnp.where(first, a + r, MMAX - 1 - a + r - first_pad).astype(F32)
    lam = degree * (degree + 1.0) / float(MMAX * (MMAX - 1))

    tr, tc = iota((trows, fl_n), 0), iota((trows, fl_n), 1)
    tfl = tr // 8 * K + tr % K
    old = jnp.concatenate([old_ref[f, 0] for f in range(3)], axis=0)
    old_rows = sum(
        dot(onehot((tfl == tc) & (tr // 4 % 2 == c)), old[:, c * nr : (c + 1) * nr]) for c in range(2)
    )

    def mid_row(i):
        i = i + first_mid
        fl = i // 8 * K + i % K
        return fl // lev_n, fl % lev_n, i // 4 % 2

    levels = nlev * lev_n

    def mode_of(i, h):
        return lev_n * ((lev + h) % nlev) + i // 2

    i1, o1 = iota((2 * half, levels), 0), iota((2 * half, levels), 1)
    pick_out = onehot((o1 == mode_of(i1 % half, i1 // half)) & (i1 % half < 2 * lev_n), F32)
    field, level, cc = mid_row(iota((levels, mid), 1))
    pick_in = onehot(iota((levels, mid), 0) == lev_n * lev + level, F32)
    field, level, cc = mid_row(iota((2 * half, mid), 1))
    same_c = iota((2 * half, mid), 0) % 2 == cc
    m_in = mi_ref[...]
    w_div = jnp.where(same_c & (field == 1), fdot(fdot(pick_out, m_in), pick_in), 0.0)
    w_heat = jnp.where(same_c & (field == 2), fdot(fdot(pick_out, fdot(m_in, g_ref[...])), pick_in), 0.0)
    w1 = jnp.concatenate([w_div, w_heat], axis=0)
    im, om = iota((half, levels), 0), iota((half, levels), 1)
    own_mode = (om == lev_n * lev + im // 2) & (im < 2 * lev_n)
    rates = jnp.sum(jnp.where(own_mode, rates_ref[...][None, :], 0.0), axis=1, keepdims=True)
    i2, l2 = iota((2 * mid, levels), 0), iota((2 * mid, levels), 1)
    field, level, cc = mid_row(i2 % mid)
    pick_lev = onehot(l2 == lev_n * ((lev + i2 // mid) % nlev) + level, F32)
    im, om = iota((levels, half), 1), iota((levels, half), 0)
    pick_mode = onehot((om == lev_n * lev + im // 2) & (im < 2 * lev_n), F32)
    field, level, cc = mid_row(iota((2 * mid, half), 0) % mid)
    same_c = iota((2 * mid, half), 1) % 2 == cc
    w2 = jnp.where(same_c & (field == 1), fdot(fdot(pick_lev, mo_ref[...]), pick_mode), 0.0)
    w2 = w2 + jnp.where(same_c & (field == 2), -2.0 * fdot(fdot(pick_lev, mh_ref[...]), pick_mode), 0.0)
    field, level, cc = mid_row(iota((mid, 1), 0))
    stays = onehot(field != 1, F32)

    loads[10].wait()

    def wait1(side):
        def step(i, carry):
            frm = peer(side, i)
            pltpu.make_async_remote_copy(
                src_ref=send1.at[frm], dst_ref=recv1.at[frm], send_sem=s1.at[frm], recv_sem=r1.at[frm],
                device_id=(frm, lev), device_id_type=MESH,
            ).wait_recv()
            return carry

        return step

    def lat_half(side):
        return pl.ds(pl.multiple_of(side * (hn * jl), 128), hn * jl)

    def forward(side):
        got = [recv1[side * hn + d] for d in range(hn)]
        cols = jnp.concatenate(
            [jnp.concatenate([m[:, g * jl : (g + 1) * jl] for m in got], axis=1) for g in range(groups)], axis=0
        )
        return lax.dot_general(cols, leg[:, lat_half(side)], NT, preferred_element_type=F32)

    lax.fori_loop(1, hn, wait1(near), 0)
    both = forward(near)
    lax.fori_loop(0, hn, wait1(far), 0)
    both = (both + forward(far)).reshape(groups, 2, 8, nr)
    total = jnp.where(iota((groups, 8, nr), 2) < first_pad, both[:, 0], both[:, 1])
    total = old_rows + jnp.where(used, total.reshape(trows, nr), 0.0)

    def exchange(src, dst, k):
        return pltpu.make_async_remote_copy(
            src_ref=src, dst_ref=dst, send_sem=es.at[k], recv_sem=er.at[k],
            device_id=(me, other), device_id_type=MESH,
        )

    tmid = total[first_mid:]
    w1s, t1s = split3(w1, tmid)
    res = dot(w1s, t1s)
    proj = res[: 2 * half] + 2.0 * lam * res[2 * half :]
    es1[...] = proj[half:].astype(BF16)
    exchange(es1, er1, 0).start()
    exchange(es1, er1, 0).wait()
    modal = (proj[:half] + er1[...].astype(F32)) / (1.0 + 4.0 * lam * rates)
    w2s, m2s = split3(w2, modal)
    res = dot(w2s, m2s)
    es2[...] = res[mid:].astype(BF16)
    exchange(es2, er2, 1).start()
    exchange(es2, er2, 1).wait()
    new_mid = tmid * stays + res[:mid] + er2[...].astype(F32)
    new = jnp.concatenate([total[:first_mid], new_mid], axis=0) if first_mid else new_mid
    new = jnp.where(used, new, 0.0)
    sides = jnp.stack(
        [
            jnp.where(first, new, 0.0).reshape(groups, 8, nr),
            jnp.where(first, 0.0, new).reshape(groups, 8, nr),
        ],
        axis=1,
    ).reshape(rows, nr).astype(BF16)

    def copy2(to):
        return pltpu.make_async_remote_copy(
            src_ref=send2.at[to], dst_ref=recv2.at[me], send_sem=s2.at[to], recv_sem=r2.at[me],
            device_id=(to, lev), device_id_type=MESH,
        )

    def start2(side):
        def step(i, carry):
            copy2(peer(side, i)).start()
            return carry

        return step

    for side, begin in ((far, 0), (near, 1)):
        grid = dot(sides, leg[:, lat_half(side)]).astype(BF16)
        for d in range(hn):
            parts = [grid[g * 16 : (g + 1) * 16, d * jl : (d + 1) * jl] for g in range(groups)]
            if lanes > groups * jl:
                parts.append(jnp.zeros((16, lanes - groups * jl), BF16))
            send2[side * hn + d] = jnp.concatenate(parts, axis=1)
        lax.fori_loop(begin, hn, start2(side), 0)
    recv2[me] = send2[me]

    new_b = new.astype(BF16)
    sr, sc = iota((fl_n, trows), 0), iota((fl_n, trows), 1)
    sfl = sc // 8 * K + sc % K
    for c in range(2):
        part = dot(onehot((sfl == sr) & (sc // 4 % 2 == c)), new_b).astype(BF16)
        for f in range(3):
            spec_ref[f, 0, :, c * nr : (c + 1) * nr] = part[f * lev_n : (f + 1) * lev_n]

    spec_copy = pltpu.make_async_copy(spec_ref, spec_hbm, out_sem.at[0])
    spec_copy.start()

    def wait2(i, carry):
        to = lax.rem(me + i, n)
        copy1(to).wait_send()
        copy2(to).wait_send()
        frm = lax.rem(me + n - i, n)
        pltpu.make_async_remote_copy(
            src_ref=send2.at[frm], dst_ref=recv2.at[frm], send_sem=s2.at[frm], recv_sem=r2.at[frm],
            device_id=(frm, lev), device_id_type=MESH,
        ).wait_recv()
        return carry

    lax.fori_loop(1, n, wait2, 0)
    out_copies = []
    perm_back = onehot(pr == pc % K * q_n + pc // K)
    back = dot(perm_back, recv2[...].reshape(K * q_n, lanes))
    for g in range(groups):
        for k in range(K):
            fl = g * K + k
            if fl < fl_n:
                piece = back[k * q_n : (k + 1) * q_n, g * jl : (g + 1) * jl] * keep
                out_ref[fl // lev_n, fl % lev_n] = piece.astype(BF16)
                if fl % lev_n == lev_n - 1:
                    f = fl // lev_n
                    out_copies.append(pltpu.make_async_copy(out_ref.at[f], out_hbm.at[f], out_sem.at[1 + f]))
                    out_copies[-1].start()
    spec_copy.wait()
    for out_copy in out_copies:
        out_copy.wait()


def body(
    fourier_in, spectral_old, legendre, g_matrix, modes_in, modes_out, mode_heating, mode_rates, pair_ids, lat_ids,
    limits,
):
    n, nlev = lax.axis_size("wave"), lax.axis_size("lev")
    fields, lev_n, jl, q_n = fourier_in.shape
    groups = (fields * lev_n + K - 1) // K
    lanes = (groups * jl + 127) // 128 * 128
    nr, nlat = legendre.shape[1:]
    half = (2 * lev_n + 15) // 16 * 16
    mid = groups * 8 - lev_n // K * 8
    hbm = pl.BlockSpec(memory_space=pltpu.HBM)
    spec, out = pl.pallas_call(
        functools.partial(kernel, n, nlev),
        out_shape=(
            jax.ShapeDtypeStruct((fields, 1, lev_n, 2 * nr), BF16),
            jax.ShapeDtypeStruct((fields, lev_n, q_n, jl), BF16),
        ),
        in_specs=[hbm] * 11,
        out_specs=(hbm, hbm),
        scratch_shapes=[
            pltpu.VMEM((fields, 1, lev_n, 2 * nr), BF16),
            pltpu.VMEM((fields, lev_n, q_n, jl), BF16),
            pltpu.VMEM((fields, lev_n, q_n, jl), BF16),
            pltpu.VMEM((fields, 1, lev_n, 2 * nr), BF16),
            pltpu.VMEM((nr, nlat), BF16),
            pltpu.VMEM(g_matrix.shape, F32),
            pltpu.VMEM(g_matrix.shape, F32),
            pltpu.VMEM(g_matrix.shape, F32),
            pltpu.VMEM(g_matrix.shape, F32),
            pltpu.VMEM(mode_rates.shape, F32),
            pltpu.SMEM(pair_ids.shape, jnp.int32),
            pltpu.VMEM(lat_ids.shape, jnp.int32),
            pltpu.VMEM(limits.shape, jnp.int32),
            pltpu.VMEM((n, 16, lanes), BF16),
            pltpu.VMEM((n, 16, lanes), BF16),
            pltpu.VMEM((n, 16, lanes), BF16),
            pltpu.VMEM((n, 16, lanes), BF16),
            pltpu.VMEM((half, nr), BF16),
            pltpu.VMEM((half, nr), BF16),
            pltpu.VMEM((mid, nr), BF16),
            pltpu.VMEM((mid, nr), BF16),
            pltpu.SemaphoreType.DMA((1 + fields,)),
            pltpu.SemaphoreType.DMA((11,)),
            pltpu.SemaphoreType.DMA((n,)),
            pltpu.SemaphoreType.DMA((n,)),
            pltpu.SemaphoreType.DMA((n,)),
            pltpu.SemaphoreType.DMA((n,)),
            pltpu.SemaphoreType.DMA((2,)),
            pltpu.SemaphoreType.DMA((2,)),
        ],
        compiler_params=pltpu.CompilerParams(
            collective_id=0, has_side_effects=True, vmem_limit_bytes=63 * 1024 * 1024
        ),
        cost_estimate=pl.CostEstimate(flops=10**9, bytes_accessed=8 * 10**6, transcendentals=0),
    )(
        jnp.transpose(fourier_in, (0, 1, 3, 2)),
        jnp.transpose(spectral_old, (0, 2, 1, 3)),
        legendre,
        g_matrix,
        modes_in,
        modes_out,
        mode_heating,
        mode_rates,
        pair_ids,
        lat_ids,
        limits,
    )
    return jnp.transpose(spec, (0, 2, 1, 3)), jnp.transpose(out, (0, 1, 3, 2))


def solution(mesh):
    wave = P(None, "lev", "wave", None)
    return jax.shard_map(
        body,
        mesh=mesh,
        in_specs=(wave, wave, P("wave", None, None)) + (P(),) * 8,
        out_specs=(wave, wave),
        check_vma=False,
    )
```

```python
import functools

import jax
import jax.numpy as jnp
from jax import lax
from jax.experimental import pallas as pl
from jax.experimental.pallas import tpu as pltpu
from jax.sharding import PartitionSpec as P

MMAX = 1280
BLOCK = 64
K = 4
F32, BF16 = jnp.float32, jnp.bfloat16
MESH = pl.DeviceIdType.MESH
HI = lax.Precision.HIGHEST
NT = (((1,), (1,)), ((), ()))


def iota(shape, dim):
    return lax.broadcasted_iota(jnp.int32, shape, dim)


def dot(a, b):
    return jnp.dot(a, b, preferred_element_type=F32)


def fdot(a, b):
    return jnp.dot(a, b, precision=HI, preferred_element_type=F32)


def onehot(mask, dtype=BF16):
    return jnp.where(mask, 1.0, 0.0).astype(dtype)


def split3(left, right):
    lh = left.astype(BF16)
    ll = (left - lh.astype(F32)).astype(BF16)
    rh = right.astype(BF16)
    rl = (right - rh.astype(F32)).astype(BF16)
    return jnp.concatenate([lh, lh, ll], axis=1), jnp.concatenate([rh, rl, rh], axis=0)


def kernel(
    n, nlev, x_hbm, old_hbm, leg_hbm, g_hbm, mi_hbm, mo_hbm, mh_hbm, rates_hbm, pid_hbm, lat_hbm, lim_hbm,
    spec_hbm, out_hbm,
    spec_ref, out_ref, x_ref, old_ref, leg, g_ref, mi_ref, mo_ref, mh_ref, rates_ref, pid_ref, lat_ref, lim_ref,
    send1, recv1, send2, recv2, es1, er1, es2, er2,
    out_sem, in_sem, s1, r1, s2, r2, es, er,
):
    lev_n = x_ref.shape[1]
    fl_n = x_ref.shape[0] * lev_n
    q_n, jl = x_ref.shape[2], x_ref.shape[3]
    groups = (fl_n + K - 1) // K
    rows = groups * 16
    trows = groups * 8
    lanes = send1.shape[2]
    nr = leg_hbm.shape[1]
    nlat = leg_hbm.shape[2]
    first_mid = lev_n // K * 8
    mid = trows - first_mid
    half = er1.shape[0]
    me, lev = lax.axis_index("wave"), lax.axis_index("lev")
    other = lax.rem(lev + 1, nlev)

    pairs = [
        (pid_hbm, pid_ref), (lat_hbm, lat_ref), (lim_hbm, lim_ref), (x_hbm, x_ref), (g_hbm, g_ref), (mi_hbm, mi_ref),
        (mo_hbm, mo_ref), (mh_hbm, mh_ref), (rates_hbm, rates_ref), (old_hbm, old_ref), (leg_hbm.at[0], leg),
    ]
    loads = [pltpu.make_async_copy(src, dst, in_sem.at[i]) for i, (src, dst) in enumerate(pairs)]
    for load in loads:
        load.start()

    barrier = pltpu.get_barrier_semaphore()

    def greet(i, carry):
        pl.semaphore_signal(barrier, inc=1, device_id=(lax.rem(me + i, n), lev), device_id_type=MESH)
        return carry

    lax.fori_loop(1, n, greet, 0)
    pl.semaphore_signal(barrier, inc=1, device_id=(me, other), device_id_type=MESH)

    for load in loads[:4]:
        load.wait()

    col = iota((jl, nlat), 1)
    own = jnp.sum(jnp.where(col == me * jl + iota((jl, nlat), 0), lat_ref[...].astype(F32)[None, :], 0.0), axis=1, keepdims=True)
    lim = jnp.sum(jnp.where(col.astype(F32) == own, lim_ref[...].astype(F32)[None, :], 0.0), axis=1, keepdims=True)
    lim = jnp.sum(jnp.where(iota((jl, jl), 0) == iota((jl, jl), 1), lim, 0.0), axis=0, keepdims=True)
    q = iota((q_n, jl), 0)
    slot = q // 4
    pair = jnp.zeros((q_n, jl), jnp.int32)
    for s in range(n):
        pair = jnp.where(slot == s, pid_ref[s], pair)
    wave = jnp.where(q // 2 % 2 == 0, pair, MMAX - 1 - pair)
    keep = onehot(wave.astype(F32) < lim, F32)

    pr, pc = iota((K * q_n, K * q_n), 0), iota((K * q_n, K * q_n), 1)
    perm = onehot(pc == pr % K * q_n + pr // K)
    keep_b = keep.astype(BF16)
    pieces = []
    for k in range(K):
        parts = []
        for g in range(groups):
            fl = g * K + k
            if fl < fl_n:
                parts.append(x_ref[fl // lev_n, fl % lev_n] * keep_b)
            else:
                parts.append(jnp.zeros((q_n, jl), BF16))
        if lanes > groups * jl:
            parts.append(jnp.zeros((q_n, lanes - groups * jl), BF16))
        pieces.append(jnp.concatenate(parts, axis=1))
    send1[...] = dot(perm, jnp.concatenate(pieces, axis=0)).astype(BF16).reshape(n, 16, lanes)

    pl.semaphore_wait(barrier, n)

    def copy1(i):
        to = lax.rem(me + i, n)
        return pltpu.make_async_remote_copy(
            src_ref=send1.at[to], dst_ref=recv1.at[me], send_sem=s1.at[to], recv_sem=r1.at[me],
            device_id=(to, lev), device_id_type=MESH,
        )

    def start1(i, carry):
        copy1(i).start()
        return carry

    lax.fori_loop(1, n, start1, 0)
    recv1[me] = send1[me]

    for load in loads[4:10]:
        load.wait()
    a = pid_ref[me]
    r = iota((1, nr), 1)
    first_pad = (MMAX - a + BLOCK - 1) // BLOCK * BLOCK
    first = r < first_pad
    used = (first & (r < MMAX - a)) | ((r >= first_pad) & (r - first_pad <= a))
    degree = jnp.where(first, a + r, MMAX - 1 - a + r - first_pad).astype(F32)
    lam = degree * (degree + 1.0) / float(MMAX * (MMAX - 1))

    tr, tc = iota((trows, fl_n), 0), iota((trows, fl_n), 1)
    tfl = tr // 8 * K + tr % K
    old = jnp.concatenate([old_ref[f, 0] for f in range(3)], axis=0)
    old_rows = sum(
        dot(onehot((tfl == tc) & (tr // 4 % 2 == c)), old[:, c * nr : (c + 1) * nr]) for c in range(2)
    )

    def mid_row(i):
        i = i + first_mid
        fl = i // 8 * K + i % K
        return fl // lev_n, fl % lev_n, i // 4 % 2

    levels = nlev * lev_n

    def mode_of(i, h):
        return lev_n * ((lev + h) % nlev) + i // 2

    i1, o1 = iota((2 * half, levels), 0), iota((2 * half, levels), 1)
    pick_out = onehot((o1 == mode_of(i1 % half, i1 // half)) & (i1 % half < 2 * lev_n), F32)
    field, level, cc = mid_row(iota((levels, mid), 1))
    pick_in = onehot(iota((levels, mid), 0) == lev_n * lev + level, F32)
    field, level, cc = mid_row(iota((2 * half, mid), 1))
    same_c = iota((2 * half, mid), 0) % 2 == cc
    m_in = mi_ref[...]
    w_div = jnp.where(same_c & (field == 1), fdot(fdot(pick_out, m_in), pick_in), 0.0)
    w_heat = jnp.where(same_c & (field == 2), fdot(fdot(pick_out, fdot(m_in, g_ref[...])), pick_in), 0.0)
    w1 = jnp.concatenate([w_div, w_heat], axis=0)
    im, om = iota((half, levels), 0), iota((half, levels), 1)
    own_mode = (om == lev_n * lev + im // 2) & (im < 2 * lev_n)
    rates = jnp.sum(jnp.where(own_mode, rates_ref[...][None, :], 0.0), axis=1, keepdims=True)
    i2, l2 = iota((2 * mid, levels), 0), iota((2 * mid, levels), 1)
    field, level, cc = mid_row(i2 % mid)
    pick_lev = onehot(l2 == lev_n * ((lev + i2 // mid) % nlev) + level, F32)
    im, om = iota((levels, half), 1), iota((levels, half), 0)
    pick_mode = onehot((om == lev_n * lev + im // 2) & (im < 2 * lev_n), F32)
    field, level, cc = mid_row(iota((2 * mid, half), 0) % mid)
    same_c = iota((2 * mid, half), 1) % 2 == cc
    w2 = jnp.where(same_c & (field == 1), fdot(fdot(pick_lev, mo_ref[...]), pick_mode), 0.0)
    w2 = w2 + jnp.where(same_c & (field == 2), -2.0 * fdot(fdot(pick_lev, mh_ref[...]), pick_mode), 0.0)
    field, level, cc = mid_row(iota((mid, 1), 0))
    stays = onehot(field != 1, F32)

    loads[10].wait()

    def wait1(i, carry):
        frm = lax.rem(me + n - i, n)
        pltpu.make_async_remote_copy(
            src_ref=send1.at[frm], dst_ref=recv1.at[frm], send_sem=s1.at[frm], recv_sem=r1.at[frm],
            device_id=(frm, lev), device_id_type=MESH,
        ).wait_recv()
        return carry

    lax.fori_loop(1, n, wait1, 0)

    cols = jnp.concatenate(
        [
            jnp.concatenate([recv1[d, :, g * jl : (g + 1) * jl] for d in range(n)], axis=1)
            for g in range(groups)
        ],
        axis=0,
    )
    both = lax.dot_general(cols, leg[...], NT, preferred_element_type=F32).reshape(groups, 2, 8, nr)
    total = jnp.where(iota((groups, 8, nr), 2) < first_pad, both[:, 0], both[:, 1])
    total = old_rows + jnp.where(used, total.reshape(trows, nr), 0.0)

    def exchange(src, dst, k):
        return pltpu.make_async_remote_copy(
            src_ref=src, dst_ref=dst, send_sem=es.at[k], recv_sem=er.at[k],
            device_id=(me, other), device_id_type=MESH,
        )

    tmid = total[first_mid:]
    w1s, t1s = split3(w1, tmid)
    res = dot(w1s, t1s)
    proj = res[: 2 * half] + 2.0 * lam * res[2 * half :]
    es1[...] = proj[half:].astype(BF16)
    exchange(es1, er1, 0).start()
    exchange(es1, er1, 0).wait()
    modal = (proj[:half] + er1[...].astype(F32)) / (1.0 + 4.0 * lam * rates)
    w2s, m2s = split3(w2, modal)
    res = dot(w2s, m2s)
    es2[...] = res[mid:].astype(BF16)
    exchange(es2, er2, 1).start()
    exchange(es2, er2, 1).wait()
    new_mid = tmid * stays + res[:mid] + er2[...].astype(F32)
    new = jnp.concatenate([total[:first_mid], new_mid], axis=0) if first_mid else new_mid
    new = jnp.where(used, new, 0.0)
    sides = jnp.stack(
        [
            jnp.where(first, new, 0.0).reshape(groups, 8, nr),
            jnp.where(first, 0.0, new).reshape(groups, 8, nr),
        ],
        axis=1,
    ).reshape(rows, nr).astype(BF16)
    grid = dot(sides, leg[...]).astype(BF16)
    for d in range(n):
        parts = [grid[g * 16 : (g + 1) * 16, d * jl : (d + 1) * jl] for g in range(groups)]
        if lanes > groups * jl:
            parts.append(jnp.zeros((16, lanes - groups * jl), BF16))
        send2[d] = jnp.concatenate(parts, axis=1)

    def copy2(i):
        to = lax.rem(me + i, n)
        return pltpu.make_async_remote_copy(
            src_ref=send2.at[to], dst_ref=recv2.at[me], send_sem=s2.at[to], recv_sem=r2.at[me],
            device_id=(to, lev), device_id_type=MESH,
        )

    def start2(i, carry):
        copy2(i).start()
        return carry

    lax.fori_loop(1, n, start2, 0)
    recv2[me] = send2[me]

    new_b = new.astype(BF16)
    sr, sc = iota((fl_n, trows), 0), iota((fl_n, trows), 1)
    sfl = sc // 8 * K + sc % K
    for c in range(2):
        part = dot(onehot((sfl == sr) & (sc // 4 % 2 == c)), new_b).astype(BF16)
        for f in range(3):
            spec_ref[f, 0, :, c * nr : (c + 1) * nr] = part[f * lev_n : (f + 1) * lev_n]

    spec_copy = pltpu.make_async_copy(spec_ref, spec_hbm, out_sem.at[0])
    spec_copy.start()

    def wait2(i, carry):
        copy1(i).wait_send()
        copy2(i).wait_send()
        frm = lax.rem(me + n - i, n)
        pltpu.make_async_remote_copy(
            src_ref=send2.at[frm], dst_ref=recv2.at[frm], send_sem=s2.at[frm], recv_sem=r2.at[frm],
            device_id=(frm, lev), device_id_type=MESH,
        ).wait_recv()
        return carry

    lax.fori_loop(1, n, wait2, 0)
    out_copies = []
    perm_back = onehot(pr == pc % K * q_n + pc // K)
    back = dot(perm_back, recv2[...].reshape(K * q_n, lanes))
    for g in range(groups):
        for k in range(K):
            fl = g * K + k
            if fl < fl_n:
                piece = back[k * q_n : (k + 1) * q_n, g * jl : (g + 1) * jl] * keep
                out_ref[fl // lev_n, fl % lev_n] = piece.astype(BF16)
                if fl % lev_n == lev_n - 1:
                    f = fl // lev_n
                    out_copies.append(pltpu.make_async_copy(out_ref.at[f], out_hbm.at[f], out_sem.at[1 + f]))
                    out_copies[-1].start()
    spec_copy.wait()
    for out_copy in out_copies:
        out_copy.wait()


def body(
    fourier_in, spectral_old, legendre, g_matrix, modes_in, modes_out, mode_heating, mode_rates, pair_ids, lat_ids,
    limits,
):
    n, nlev = lax.axis_size("wave"), lax.axis_size("lev")
    fields, lev_n, jl, q_n = fourier_in.shape
    groups = (fields * lev_n + K - 1) // K
    lanes = (groups * jl + 127) // 128 * 128
    nr, nlat = legendre.shape[1:]
    half = (2 * lev_n + 15) // 16 * 16
    mid = groups * 8 - lev_n // K * 8
    hbm = pl.BlockSpec(memory_space=pltpu.HBM)
    spec, out = pl.pallas_call(
        functools.partial(kernel, n, nlev),
        out_shape=(
            jax.ShapeDtypeStruct((fields, 1, lev_n, 2 * nr), BF16),
            jax.ShapeDtypeStruct((fields, lev_n, q_n, jl), BF16),
        ),
        in_specs=[hbm] * 11,
        out_specs=(hbm, hbm),
        scratch_shapes=[
            pltpu.VMEM((fields, 1, lev_n, 2 * nr), BF16),
            pltpu.VMEM((fields, lev_n, q_n, jl), BF16),
            pltpu.VMEM((fields, lev_n, q_n, jl), BF16),
            pltpu.VMEM((fields, 1, lev_n, 2 * nr), BF16),
            pltpu.VMEM((nr, nlat), BF16),
            pltpu.VMEM(g_matrix.shape, F32),
            pltpu.VMEM(g_matrix.shape, F32),
            pltpu.VMEM(g_matrix.shape, F32),
            pltpu.VMEM(g_matrix.shape, F32),
            pltpu.VMEM(mode_rates.shape, F32),
            pltpu.SMEM(pair_ids.shape, jnp.int32),
            pltpu.VMEM(lat_ids.shape, jnp.int32),
            pltpu.VMEM(limits.shape, jnp.int32),
            pltpu.VMEM((n, 16, lanes), BF16),
            pltpu.VMEM((n, 16, lanes), BF16),
            pltpu.VMEM((n, 16, lanes), BF16),
            pltpu.VMEM((n, 16, lanes), BF16),
            pltpu.VMEM((half, nr), BF16),
            pltpu.VMEM((half, nr), BF16),
            pltpu.VMEM((mid, nr), BF16),
            pltpu.VMEM((mid, nr), BF16),
            pltpu.SemaphoreType.DMA((1 + fields,)),
            pltpu.SemaphoreType.DMA((11,)),
            pltpu.SemaphoreType.DMA((n,)),
            pltpu.SemaphoreType.DMA((n,)),
            pltpu.SemaphoreType.DMA((n,)),
            pltpu.SemaphoreType.DMA((n,)),
            pltpu.SemaphoreType.DMA((2,)),
            pltpu.SemaphoreType.DMA((2,)),
        ],
        compiler_params=pltpu.CompilerParams(
            collective_id=0, has_side_effects=True, vmem_limit_bytes=63 * 1024 * 1024
        ),
        cost_estimate=pl.CostEstimate(flops=10**9, bytes_accessed=8 * 10**6, transcendentals=0),
    )(
        jnp.transpose(fourier_in, (0, 1, 3, 2)),
        jnp.transpose(spectral_old, (0, 2, 1, 3)),
        legendre,
        g_matrix,
        modes_in,
        modes_out,
        mode_heating,
        mode_rates,
        pair_ids,
        lat_ids,
        limits,
    )
    return jnp.transpose(spec, (0, 2, 1, 3)), jnp.transpose(out, (0, 1, 3, 2))


def solution(mesh):
    wave = P(None, "lev", "wave", None)
    return jax.shard_map(
        body,
        mesh=mesh,
        in_specs=(wave, wave, P("wave", None, None)) + (P(),) * 8,
        out_specs=(wave, wave),
        check_vma=False,
    )
```
